32 devices in a mesh: token: 4 (over z), head: 4 (over x, core), image: 2 (over y).
Axes of the slice: x: 2, y: 2, z: 4, core: 2. Of those that a mesh axis runs over, the one named last changes fastest.
Arguments:
- queries: bfloat16 [32, 80, 2048], P(('image', 'head'), None, 'token'), parts along dimension 0, may hold values from -6 to 6
- keys: bfloat16 [32, 80, 2048], P(('image', 'head'), None, 'token'), parts along dimension 0, may hold values from -6 to 6
- values: bfloat16 [32, 80, 2048], P(('image', 'head'), None, 'token'), parts along dimension 0, may hold values from -6 to 6
- out_grad: bfloat16 [32, 80, 2048], P(('image', 'head'), None, 'token'), parts along dimension 0, may hold values from -6 to 6
- flags: int32 [4, 4], replicated, may hold values from 0 to 1, as said below
- order: int32 [4], replicated, may hold values from 0 to 3, each once
Outputs:
- attended: bfloat16 [32, 80, 2048], P(('image', 'head'), None, 'token'), parts along dimension 0
- query_grad: bfloat16 [32, 80, 2048], P(('image', 'head'), None, 'token'), parts along dimension 0
- key_grad: bfloat16 [32, 80, 2048], P(('image', 'head'), None, 'token'), parts along dimension 0
- value_grad: bfloat16 [32, 80, 2048], P(('image', 'head'), None, 'token'), parts along dimension 0
The draws below stay inside these ranges and needn't reach their ends.
There are 2 independent parts, one for each index of `image`. The reference program is written for one: setup_inputs(seed, part) draws one part's arguments, and reference() takes and returns one part's arrays. A program takes and returns all parts, laid end to end along the dimension named above; an argument that names none is the same for every part. Nothing has to cross between parts.
Inputs may be any that keep to these rules, and one draw needn't show every extreme that they name: `flags`: every image block may attend to itself. `order`: each image block once.
All inputs are finite; a program needn't handle non-finite values.
Results may differ from the reference program's by a relative error of at most 0.017.
Values may be sent and summed in bfloat16 or wider, within the bound.
A program may use at most 64 MiB of HBM per device.

```python
import jax
import jax.numpy as jnp
from jax import lax

HEADS = 16
HEAD_DIM = 80
BLK = 512
TOKENS = 2048
NB = 4


def draw_queries(key, part):
    key = jax.random.fold_in(key, 1)
    base = 1.8 * jnp.clip(jax.random.normal(key, (HEADS, HEAD_DIM, TOKENS), jnp.float32), -3.3, 3.3)
    return base.astype(jnp.bfloat16)


def draw_keys(key, part):
    key = jax.random.fold_in(key, 2)
    base = 1.8 * jnp.clip(jax.random.normal(key, (HEADS, HEAD_DIM, TOKENS), jnp.float32), -3.3, 3.3)
    return base.astype(jnp.bfloat16)


def draw_flags(key, part):
    key = jax.random.fold_in(key, 5)
    first, second = jax.random.split(key)
    rows = jnp.arange(NB, dtype=jnp.int32)[:, None]
    cols = jnp.arange(NB, dtype=jnp.int32)[None, :]
    band = jnp.abs(rows - cols) <= 1
    center = jax.random.randint(first, (), 0, NB)
    extra = jax.random.randint(second, (NB, NB), 0, NB) == 0
    return (band | (rows == center) | (cols == center) | extra).astype(jnp.int32)


def level_of(own_key, dims, pieces, least, largest):
    gain, own = 1.0, jax.random.fold_in(own_key, 6)
    for dim, parts in pieces:
        heights = jnp.exp(jax.random.uniform(jax.random.fold_in(own, dim), (parts,), jnp.float32, least / len(pieces), largest / len(pieces)))
        gain = gain * jnp.repeat(heights, dims[dim] // parts).reshape([-1 if axis == dim else 1 for axis in range(len(dims))])
    return gain


def scatter_about(key, dims, width, bound, cuts=(), kind=jnp.bfloat16):
    level = level_of(key, dims, cuts, -0.22, 0.18) if cuts else 1.0
    entries = jax.random.normal(key, dims, jnp.float32) * width * level
    return jnp.minimum(jnp.maximum(entries, -bound), bound).astype(kind)


def setup_inputs(seed: int = 0, part: int = 0) -> dict:
    splits = jax.random.split(jax.random.key(seed), 7)
    part_splits = jax.random.split(jax.random.fold_in(splits[6], part), 7)
    queries = draw_queries(jax.random.fold_in(jax.random.fold_in(splits[6], part), 71), part)
    keys = draw_keys(jax.random.fold_in(jax.random.fold_in(splits[6], part), 71), part)
    values = scatter_about(part_splits[2], (HEADS, HEAD_DIM, TOKENS), 1.0, 6.0, ((0, 4), (2, 4)))
    out_grad = scatter_about(part_splits[3], (HEADS, HEAD_DIM, TOKENS), 1.0, 6.0, ((0, 4), (2, 4)))
    flags = draw_flags(jax.random.fold_in(splits[6], 71), part)
    order = jax.random.permutation(splits[5], NB).astype(jnp.int32)
    return {"queries": queries, "keys": keys, "values": values, "out_grad": out_grad, "flags": flags, "order": order}


def reference(queries, keys, values, out_grad, flags, order):
    nblk = order.shape[0]
    onehot = (order[:, None] == jnp.arange(nblk, dtype=jnp.int32)[None, :]).astype(jnp.float32)
    block_ok = jnp.dot(jnp.dot(onehot, flags.astype(jnp.float32)), onehot.T) > 0.5
    allowed = jnp.repeat(jnp.repeat(block_ok, BLK, axis=0), BLK, axis=1)
    scale = HEAD_DIM ** -0.5

    def one_head(arrays):
        query, key, value, grad = arrays
        score = jnp.dot(query.T, key, preferred_element_type=jnp.float32) * scale
        score = jnp.where(allowed, score, -jnp.inf)
        rowmax = jnp.max(score, axis=1, keepdims=True)
        weight = jnp.exp(score - rowmax)
        total = jnp.sum(weight, axis=1)
        attended = (jnp.dot(weight.astype(jnp.bfloat16), value.T, preferred_element_type=jnp.float32) / total[:, None]).astype(jnp.bfloat16)
        lse = rowmax[:, 0] + jnp.log(total)
        prob = jnp.exp(score - lse[:, None])
        delta = jnp.sum(grad.T.astype(jnp.float32) * attended.astype(jnp.float32), axis=1)
        value_grad = jnp.dot(prob.astype(jnp.bfloat16).T, grad.T, preferred_element_type=jnp.float32)
        dprob = jnp.dot(grad.T, value, preferred_element_type=jnp.float32)
        dscore = (prob * (dprob - delta[:, None]) * scale).astype(jnp.bfloat16)
        query_grad = jnp.dot(dscore, key.T, preferred_element_type=jnp.float32)
        key_grad = jnp.dot(dscore.T, query.T, preferred_element_type=jnp.float32)
        return (attended.T, query_grad.T.astype(jnp.bfloat16), key_grad.T.astype(jnp.bfloat16), value_grad.T.astype(jnp.bfloat16))

    attended, query_grad, key_grad, value_grad = lax.map(one_head, (queries, keys, values, out_grad))
    return (attended, query_grad, key_grad, value_grad)
```

```python
import functools

import jax
import jax.numpy as jnp
from jax import lax
from jax.experimental import pallas as pl
from jax.experimental.pallas import tpu as pltpu
from jax.sharding import PartitionSpec as P

BLK = 512


def from_behind(value, axis, steps):
    count = lax.axis_size(axis)
    pairs = [(source, (source + steps) % count) for source in range(count)]
    return lax.ppermute(value, axis, pairs)


def block_pairs(flags, order, query_dev, key_dev, per):
    nblk = order.shape[0]
    labels = jnp.arange(nblk, dtype=jnp.int32)[None, :]
    query_ids = lax.dynamic_slice_in_dim(order, query_dev * per, per)
    key_ids = lax.dynamic_slice_in_dim(order, key_dev * per, per)
    query_hot = (query_ids[:, None] == labels).astype(jnp.float32)
    key_hot = (key_ids[:, None] == labels).astype(jnp.float32)
    return jnp.dot(jnp.dot(query_hot, flags.astype(jnp.float32)), key_hot.T) > 0.5


def masked_scores(query, key, pairs, scale):
    score = jnp.einsum("hdi,hdj->hij", query, key, preferred_element_type=jnp.float32) * scale
    heads, rows, cols = score.shape
    per = pairs.shape[0]
    shaped = score.reshape(heads, per, rows // per, per, cols // per)
    shaped = jnp.where(pairs[None, :, None, :, None], shaped, -jnp.inf)
    return shaped.reshape(heads, rows, cols)


def forward_tile(query, key, value, state, pairs, scale):
    output, running_max, total = state
    score = masked_scores(query, key, pairs, scale)
    new_max = jnp.maximum(running_max, jnp.max(score, axis=2))
    safe_max = jnp.where(jnp.isfinite(new_max), new_max, 0.0)
    rescale = jnp.exp(running_max - safe_max)
    weight = jnp.exp(score - safe_max[..., None])
    total = total * rescale + jnp.sum(weight, axis=2)
    output = output * rescale[:, None, :] + jnp.einsum(
        "hij,hdj->hdi", weight.astype(jnp.bfloat16), value, preferred_element_type=jnp.float32
    )
    return (output, new_max, total)


def backward_tile(query, grad, lse, delta, key, value, pairs, scale):
    score = masked_scores(query, key, pairs, scale)
    prob = jnp.exp(score - lse[..., None])
    value_part = jnp.einsum(
        "hij,hdi->hdj", prob.astype(jnp.bfloat16), grad, preferred_element_type=jnp.float32
    )
    dprob = jnp.einsum("hdi,hdj->hij", grad, value, preferred_element_type=jnp.float32)
    dscore = (prob * (dprob - delta[..., None]) * scale).astype(jnp.bfloat16)
    key_part = jnp.einsum("hij,hdi->hdj", dscore, query, preferred_element_type=jnp.float32)
    query_part = jnp.einsum("hij,hdj->hdi", dscore, key, preferred_element_type=jnp.float32)
    return (query_part, key_part, value_part)


def ring_body(queries, keys, values, out_grad, flags, order):
    cycle = lax.axis_size("token")
    me = lax.axis_index("token")
    heads, dim, toks = queries.shape
    per = toks // BLK
    scale = dim ** (-0.5)
    zero_field = jnp.zeros((heads, dim, toks), jnp.float32)
    zero_rows = jnp.zeros((heads, toks), jnp.float32)
    start_max = jnp.full((heads, toks), -jnp.inf, jnp.float32)

    def forward_step(step, carry):
        visitor, output, running_max, total = carry
        source = (me - step) % cycle
        pairs = block_pairs(flags, order, source, me, per)
        state = lax.cond(
            jnp.any(pairs),
            lambda s: forward_tile(visitor, keys, values, s, pairs, scale),
            lambda s: s,
            (output, running_max, total),
        )
        visitor = from_behind(visitor, "token", 1)
        output, running_max, total = from_behind(state, "token", 1)
        return (visitor, output, running_max, total)

    _, output, running_max, total = lax.fori_loop(
        0, cycle, forward_step, (queries, zero_field, start_max, zero_rows)
    )
    state = (output, running_max, total)
    finish_output, finish_running_max, finish_total = state
    attended = (finish_output / finish_total[:, None, :]).astype(jnp.bfloat16)
    lse = finish_running_max + jnp.log(finish_total)
    delta = jnp.sum(out_grad.astype(jnp.float32) * attended.astype(jnp.float32), axis=1)
    attended, lse, delta = (attended, lse, delta)

    def backward_step(step, carry):
        visitor, grad, query_acc, lse_vis, delta_vis, key_acc, value_acc = carry
        source = (me - step) % cycle
        pairs = block_pairs(flags, order, source, me, per)

        def live(accs):
            query_part, key_part, value_part = backward_tile(
                visitor, grad, lse_vis, delta_vis, keys, values, pairs, scale
            )
            return (accs[0] + query_part, accs[1] + key_part, accs[2] + value_part)

        query_acc, key_acc, value_acc = lax.cond(
            jnp.any(pairs), live, lambda a: a, (query_acc, key_acc, value_acc)
        )
        visitor, grad = from_behind((visitor, grad), "token", 1)
        query_acc, lse_vis, delta_vis = from_behind((query_acc, lse_vis, delta_vis), "token", 1)
        return (visitor, grad, query_acc, lse_vis, delta_vis, key_acc, value_acc)

    final = lax.fori_loop(
        0, cycle, backward_step, (queries, out_grad, zero_field, lse, delta, zero_field, zero_field)
    )
    query_acc, key_acc, value_acc = (final[2], final[5], final[6])
    return (
        attended,
        query_acc.astype(jnp.bfloat16),
        key_acc.astype(jnp.bfloat16),
        value_acc.astype(jnp.bfloat16),
    )


NT = (((1,), (1,)), ((), ()))
LOG2E = 1.4426950408889634
SUB = 256


def dot(a, b):
    return jnp.dot(a, b, preferred_element_type=jnp.float32)


def dot_nt(a, b):
    return lax.dot_general(a, b, NT, preferred_element_type=jnp.float32)


def swap_kernel(
    n, flags, order, q_in, k_in, v_in, g_in, o_out, dq_out, dk_out, dv_out,
    qb, kb, vb, gb, kt, vt, score, prob, dk_acc, dv_acc, ob, dqb, dkb, dvb,
    in_send, in_recv, out_send, out_recv,
):
    me = lax.axis_index("token")
    dim, blk = qb.shape[1:]
    scale = dim ** (-0.5)
    expo = scale * LOG2E
    ins = ((k_in, kb), (v_in, vb), (q_in, qb), (g_in, gb))
    outs = ((ob, o_out), (dqb, dq_out), (dkb, dk_out), (dvb, dv_out))
    offs = [n // 2] + [o for o in range(1, n) if o != n // 2]

    def other(off):
        return lax.rem(me + off, n)

    def send_in(t, off):
        src, dst = ins[t]
        to = other(off)
        return pltpu.make_async_remote_copy(
            src_ref=src.at[to], dst_ref=dst.at[me], send_sem=in_send.at[t, off],
            recv_sem=in_recv.at[t, me], device_id={"token": to},
        )

    def take_in(t, frm):
        src, dst = ins[t]
        return pltpu.make_async_remote_copy(
            src_ref=src.at[me], dst_ref=dst.at[frm], send_sem=in_send.at[t, 0],
            recv_sem=in_recv.at[t, frm], device_id={"token": frm},
        )

    def own_in(t):
        src, dst = ins[t]
        return pltpu.make_async_copy(src.at[me], dst.at[me], in_recv.at[t, me])

    def send_out(t, to):
        src, dst = outs[t]
        return pltpu.make_async_remote_copy(
            src_ref=src.at[to], dst_ref=dst.at[me], send_sem=out_send.at[t, to],
            recv_sem=out_recv.at[t, me], device_id={"token": to},
        )

    def take_out(t, frm):
        src, dst = outs[t]
        return pltpu.make_async_remote_copy(
            src_ref=src.at[me], dst_ref=dst.at[frm], send_sem=out_send.at[t, me],
            recv_sem=out_recv.at[t, frm], device_id={"token": frm},
        )

    def own_out(t):
        src, dst = outs[t]
        return pltpu.make_async_copy(src.at[me], dst.at[me], out_recv.at[t, me])

    for t in range(4):
        own_in(t).start()
    barrier = pltpu.get_barrier_semaphore()
    for off in range(1, n):
        pl.semaphore_signal(barrier, inc=1, device_id={"token": other(off)})
    pl.semaphore_wait(barrier, n - 1)

    for t in range(2):
        for off in offs:
            send_in(t, off).start()
    dk_acc[...] = jnp.zeros_like(dk_acc)
    dv_acc[...] = jnp.zeros_like(dv_acc)
    for t in range(4):
        own_in(t).wait()
    for off in offs:
        send_in(0, off).wait_send()
    for off in offs:
        for t in (2, 3):
            send_in(t, off).start()
    for off in offs:
        take_in(0, other(off)).wait_recv()
    for j in range(n):
        kt[j] = kb[j].astype(jnp.float32).T.astype(jnp.bfloat16)
    for off in offs:
        take_in(1, other(off)).wait_recv()
    for j in range(n):
        vt[j] = vb[j].astype(jnp.float32).T.astype(jnp.bfloat16)

    parts = blk // SUB

    def step(i, carry):
        turn, sub = i // parts, lax.rem(i, parts)
        off = jnp.where(turn == 0, 0, jnp.where(turn == 1, n // 2, jnp.where(turn <= n // 2, turn - 1, turn)))
        row = other(off)
        cols = pl.ds(pl.multiple_of(sub * SUB, SUB), SUB)

        @pl.when(jnp.logical_and(turn > 0, sub == 0))
        def _():
            take_in(2, row).wait_recv()
            take_in(3, row).wait_recv()

        label = order[row]
        bias = [jnp.where(flags[label, order[j]] != 0, 0.0, -jnp.inf) for j in range(n)]
        q = qb[row, :, cols]
        g = gb[row, :, cols]
        top = None
        for j in range(n):
            s = dot(kt[j], q)
            score[j] = s
            m = jnp.max(s, axis=0, keepdims=True) + bias[j]
            top = m if top is None else jnp.maximum(top, m)
        top = top * expo
        total = jnp.zeros_like(top)
        o = jnp.zeros((dim, SUB), jnp.float32)
        for j in range(n):
            p = jnp.exp2(score[j] * expo - (top - bias[j]))
            total += jnp.sum(p, axis=0, keepdims=True)
            low = p.astype(jnp.bfloat16)
            prob[j] = low
            o += dot(vb[j], low)
        inv = 1.0 / total
        att = (o * inv).astype(jnp.bfloat16)
        ob[row, :, cols] = att
        gf = g.astype(jnp.float32)
        delta = jnp.sum(gf * att.astype(jnp.float32), axis=0, keepdims=True)
        gs = (gf * inv).astype(jnp.bfloat16)
        qs = (q.astype(jnp.float32) * (inv * scale)).astype(jnp.bfloat16)
        dq = jnp.zeros((dim, SUB), jnp.float32)
        for j in range(n):
            low = prob[j]
            dp = dot(vt[j], g)
            ds = (low.astype(jnp.float32) * (dp - delta)).astype(jnp.bfloat16)
            dv_acc[j] += dot_nt(gs, low)
            dk_acc[j] += dot_nt(qs, ds)
            dq += dot(kb[j], ds)
        dqb[row, :, cols] = (dq * (inv * scale)).astype(jnp.bfloat16)

        @pl.when(jnp.logical_and(turn == 0, sub == parts - 1))
        def _():
            for t in range(2):
                own_out(t).start()

        @pl.when(jnp.logical_and(turn > 0, sub == parts - 1))
        def _():
            for t in range(2):
                send_out(t, row).start()

        return carry

    lax.fori_loop(0, n * parts, step, 0)

    dkb[...] = dk_acc[...].astype(jnp.bfloat16)
    dvb[...] = dv_acc[...].astype(jnp.bfloat16)
    for off in offs:
        for t in (2, 3):
            send_out(t, other(off)).start()
    for t in (2, 3):
        own_out(t).start()
    for t in range(1, 4):
        for off in offs:
            send_in(t, off).wait_send()
    for t in range(4):
        own_out(t).wait()
        for off in offs:
            send_out(t, other(off)).wait_send()
            take_out(t, other(off)).wait_recv()


def swap_body(queries, keys, values, out_grad, flags, order):
    n = lax.axis_size("token")
    heads, dim, blk = queries.shape
    low = pltpu.VMEM((n, dim, blk), jnp.bfloat16)
    wide = pltpu.VMEM((n, dim, blk), jnp.float32)
    turned = pltpu.VMEM((n, blk, dim), jnp.bfloat16)
    anywhere = pl.BlockSpec(memory_space=pl.ANY)
    smem = pl.BlockSpec(memory_space=pltpu.SMEM)
    sems = pltpu.SemaphoreType.DMA((4, n))
    toks = n * blk
    return tuple(
        pl.pallas_call(
            functools.partial(swap_kernel, n),
            out_shape=[jax.ShapeDtypeStruct(queries.shape, jnp.bfloat16)] * 4,
            in_specs=[smem, smem] + [anywhere] * 4,
            out_specs=[anywhere] * 4,
            scratch_shapes=[low] * 4
            + [turned] * 2
            + [pltpu.VMEM((n, blk, SUB), jnp.float32), pltpu.VMEM((n, blk, SUB), jnp.bfloat16)]
            + [wide] * 2
            + [low] * 4
            + [sems] * 4,
            compiler_params=pltpu.CompilerParams(
                collective_id=0, has_side_effects=True, vmem_limit_bytes=40 * 1024 * 1024
            ),
            cost_estimate=pl.CostEstimate(
                flops=12 * dim * toks * toks, bytes_accessed=16 * heads * dim * blk,
                transcendentals=toks * toks,
            ),
        )(flags, order, queries, keys, values, out_grad)
    )


def body(queries, keys, values, out_grad, flags, order):
    n = lax.axis_size("token")
    heads, _, toks = queries.shape
    if n > 1 and n % 2 == 0 and heads == n and toks == BLK:
        return swap_body(queries, keys, values, out_grad, flags, order)
    return ring_body(queries, keys, values, out_grad, flags, order)


def solution(mesh):
    in_specs = (
        P(("image", "head"), None, "token"),
        P(("image", "head"), None, "token"),
        P(("image", "head"), None, "token"),
        P(("image", "head"), None, "token"),
        P(),
        P(),
    )
    out_specs = (
        P(("image", "head"), None, "token"),
        P(("image", "head"), None, "token"),
        P(("image", "head"), None, "token"),
        P(("image", "head"), None, "token"),
    )
    return jax.shard_map(body, mesh=mesh, in_specs=in_specs, out_specs=out_specs, check_vma=False)
```

```python
import functools

import jax
import jax.numpy as jnp
from jax import lax
from jax.experimental import pallas as pl
from jax.experimental.pallas import tpu as pltpu
from jax.sharding import PartitionSpec as P

BLK = 512


def from_behind(value, axis, steps):
    count = lax.axis_size(axis)
    pairs = [(source, (source + steps) % count) for source in range(count)]
    return lax.ppermute(value, axis, pairs)


def block_pairs(flags, order, query_dev, key_dev, per):
    nblk = order.shape[0]
    labels = jnp.arange(nblk, dtype=jnp.int32)[None, :]
    query_ids = lax.dynamic_slice_in_dim(order, query_dev * per, per)
    key_ids = lax.dynamic_slice_in_dim(order, key_dev * per, per)
    query_hot = (query_ids[:, None] == labels).astype(jnp.float32)
    key_hot = (key_ids[:, None] == labels).astype(jnp.float32)
    return jnp.dot(jnp.dot(query_hot, flags.astype(jnp.float32)), key_hot.T) > 0.5


def masked_scores(query, key, pairs, scale):
    score = jnp.einsum("hdi,hdj->hij", query, key, preferred_element_type=jnp.float32) * scale
    heads, rows, cols = score.shape
    per = pairs.shape[0]
    shaped = score.reshape(heads, per, rows // per, per, cols // per)
    shaped = jnp.where(pairs[None, :, None, :, None], shaped, -jnp.inf)
    return shaped.reshape(heads, rows, cols)


def forward_tile(query, key, value, state, pairs, scale):
    output, running_max, total = state
    score = masked_scores(query, key, pairs, scale)
    new_max = jnp.maximum(running_max, jnp.max(score, axis=2))
    safe_max = jnp.where(jnp.isfinite(new_max), new_max, 0.0)
    rescale = jnp.exp(running_max - safe_max)
    weight = jnp.exp(score - safe_max[..., None])
    total = total * rescale + jnp.sum(weight, axis=2)
    output = output * rescale[:, None, :] + jnp.einsum(
        "hij,hdj->hdi", weight.astype(jnp.bfloat16), value, preferred_element_type=jnp.float32
    )
    return (output, new_max, total)


def backward_tile(query, grad, lse, delta, key, value, pairs, scale):
    score = masked_scores(query, key, pairs, scale)
    prob = jnp.exp(score - lse[..., None])
    value_part = jnp.einsum(
        "hij,hdi->hdj", prob.astype(jnp.bfloat16), grad, preferred_element_type=jnp.float32
    )
    dprob = jnp.einsum("hdi,hdj->hij", grad, value, preferred_element_type=jnp.float32)
    dscore = (prob * (dprob - delta[..., None]) * scale).astype(jnp.bfloat16)
    key_part = jnp.einsum("hij,hdi->hdj", dscore, query, preferred_element_type=jnp.float32)
    query_part = jnp.einsum("hij,hdj->hdi", dscore, key, preferred_element_type=jnp.float32)
    return (query_part, key_part, value_part)


def ring_body(queries, keys, values, out_grad, flags, order):
    cycle = lax.axis_size("token")
    me = lax.axis_index("token")
    heads, dim, toks = queries.shape
    per = toks // BLK
    scale = dim ** (-0.5)
    zero_field = jnp.zeros((heads, dim, toks), jnp.float32)
    zero_rows = jnp.zeros((heads, toks), jnp.float32)
    start_max = jnp.full((heads, toks), -jnp.inf, jnp.float32)

    def forward_step(step, carry):
        visitor, output, running_max, total = carry
        source = (me - step) % cycle
        pairs = block_pairs(flags, order, source, me, per)
        state = lax.cond(
            jnp.any(pairs),
            lambda s: forward_tile(visitor, keys, values, s, pairs, scale),
            lambda s: s,
            (output, running_max, total),
        )
        visitor = from_behind(visitor, "token", 1)
        output, running_max, total = from_behind(state, "token", 1)
        return (visitor, output, running_max, total)

    _, output, running_max, total = lax.fori_loop(
        0, cycle, forward_step, (queries, zero_field, start_max, zero_rows)
    )
    state = (output, running_max, total)
    finish_output, finish_running_max, finish_total = state
    attended = (finish_output / finish_total[:, None, :]).astype(jnp.bfloat16)
    lse = finish_running_max + jnp.log(finish_total)
    delta = jnp.sum(out_grad.astype(jnp.float32) * attended.astype(jnp.float32), axis=1)
    attended, lse, delta = (attended, lse, delta)

    def backward_step(step, carry):
        visitor, grad, query_acc, lse_vis, delta_vis, key_acc, value_acc = carry
        source = (me - step) % cycle
        pairs = block_pairs(flags, order, source, me, per)

        def live(accs):
            query_part, key_part, value_part = backward_tile(
                visitor, grad, lse_vis, delta_vis, keys, values, pairs, scale
            )
            return (accs[0] + query_part, accs[1] + key_part, accs[2] + value_part)

        query_acc, key_acc, value_acc = lax.cond(
            jnp.any(pairs), live, lambda a: a, (query_acc, key_acc, value_acc)
        )
        visitor, grad = from_behind((visitor, grad), "token", 1)
        query_acc, lse_vis, delta_vis = from_behind((query_acc, lse_vis, delta_vis), "token", 1)
        return (visitor, grad, query_acc, lse_vis, delta_vis, key_acc, value_acc)

    final = lax.fori_loop(
        0, cycle, backward_step, (queries, out_grad, zero_field, lse, delta, zero_field, zero_field)
    )
    query_acc, key_acc, value_acc = (final[2], final[5], final[6])
    return (
        attended,
        query_acc.astype(jnp.bfloat16),
        key_acc.astype(jnp.bfloat16),
        value_acc.astype(jnp.bfloat16),
    )


NT = (((1,), (1,)), ((), ()))
LOG2E = 1.4426950408889634
SUB = 256


def dot(a, b):
    return jnp.dot(a, b, preferred_element_type=jnp.float32)


def dot_nt(a, b):
    return lax.dot_general(a, b, NT, preferred_element_type=jnp.float32)


def swap_kernel(
    n, flags, order, q_in, k_in, v_in, g_in, o_out, dq_out, dk_out, dv_out,
    qb, kb, vb, gb, kt, vt, score, prob, dk_acc, dv_acc, ob, dqb, dkb, dvb,
    in_send, in_recv, out_send, out_recv,
):
    me = lax.axis_index("token")
    dim, blk = qb.shape[1:]
    scale = dim ** (-0.5)
    expo = scale * LOG2E
    ins = ((k_in, kb), (v_in, vb), (q_in, qb), (g_in, gb))
    outs = ((ob, o_out), (dqb, dq_out), (dkb, dk_out), (dvb, dv_out))
    offs = [n // 2] + [o for o in range(1, n) if o != n // 2]

    def other(off):
        return lax.rem(me + off, n)

    def send_in(t, off):
        src, dst = ins[t]
        to = other(off)
        return pltpu.make_async_remote_copy(
            src_ref=src.at[to], dst_ref=dst.at[me], send_sem=in_send.at[t, off],
            recv_sem=in_recv.at[t, me], device_id={"token": to},
        )

    def take_in(t, frm):
        src, dst = ins[t]
        return pltpu.make_async_remote_copy(
            src_ref=src.at[me], dst_ref=dst.at[frm], send_sem=in_send.at[t, 0],
            recv_sem=in_recv.at[t, frm], device_id={"token": frm},
        )

    def own_in(t):
        src, dst = ins[t]
        return pltpu.make_async_copy(src.at[me], dst.at[me], in_recv.at[t, me])

    def send_out(t, to):
        src, dst = outs[t]
        return pltpu.make_async_remote_copy(
            src_ref=src.at[to], dst_ref=dst.at[me], send_sem=out_send.at[t, to],
            recv_sem=out_recv.at[t, me], device_id={"token": to},
        )

    def take_out(t, frm):
        src, dst = outs[t]
        return pltpu.make_async_remote_copy(
            src_ref=src.at[me], dst_ref=dst.at[frm], send_sem=out_send.at[t, me],
            recv_sem=out_recv.at[t, frm], device_id={"token": frm},
        )

    def own_out(t):
        src, dst = outs[t]
        return pltpu.make_async_copy(src.at[me], dst.at[me], out_recv.at[t, me])

    for t in range(4):
        own_in(t).start()
    barrier = pltpu.get_barrier_semaphore()
    for off in range(1, n):
        pl.semaphore_signal(barrier, inc=1, device_id={"token": other(off)})
    pl.semaphore_wait(barrier, n - 1)

    for t in range(2):
        for off in offs:
            send_in(t, off).start()
    dk_acc[...] = jnp.zeros_like(dk_acc)
    dv_acc[...] = jnp.zeros_like(dv_acc)
    for t in range(4):
        own_in(t).wait()
    for off in offs:
        send_in(0, off).wait_send()
    for off in offs:
        for t in (2, 3):
            send_in(t, off).start()
    for off in offs:
        take_in(0, other(off)).wait_recv()
    for j in range(n):
        kt[j] = kb[j].astype(jnp.float32).T.astype(jnp.bfloat16)
    for off in offs:
        take_in(1, other(off)).wait_recv()
    for j in range(n):
        vt[j] = vb[j].astype(jnp.float32).T.astype(jnp.bfloat16)

    parts = blk // SUB

    def step(i, carry):
        turn, sub = i // parts, lax.rem(i, parts)
        off = jnp.where(turn == 0, 0, jnp.where(turn == 1, n // 2, jnp.where(turn <= n // 2, turn - 1, turn)))
        row = other(off)
        cols = pl.ds(pl.multiple_of(sub * SUB, SUB), SUB)

        @pl.when(jnp.logical_and(turn > 0, sub == 0))
        def _():
            take_in(2, row).wait_recv()
            take_in(3, row).wait_recv()

        label = order[row]
        bias = [jnp.where(flags[label, order[j]] != 0, 0.0, -jnp.inf) for j in range(n)]
        q = qb[row, :, cols]
        g = gb[row, :, cols]
        top = None
        for j in range(n):
            s = dot(kt[j], q)
            score[j] = s
            m = jnp.max(s, axis=0, keepdims=True) + bias[j]
            top = m if top is None else jnp.maximum(top, m)
        top = top * expo
        total = jnp.zeros_like(top)
        o = jnp.zeros((dim, SUB), jnp.float32)
        for j in range(n):
            p = jnp.exp2(score[j] * expo - (top - bias[j]))
            total += jnp.sum(p, axis=0, keepdims=True)
            low = p.astype(jnp.bfloat16)
            prob[j] = low
            o += dot(vb[j], low)
        inv = 1.0 / total
        att = (o * inv).astype(jnp.bfloat16)
        ob[row, :, cols] = att
        gf = g.astype(jnp.float32)
        delta = jnp.sum(gf * att.astype(jnp.float32), axis=0, keepdims=True)
        gs = (gf * inv).astype(jnp.bfloat16)
        qs = (q.astype(jnp.float32) * (inv * scale)).astype(jnp.bfloat16)
        dq = jnp.zeros((dim, SUB), jnp.float32)
        for j in range(n):
            low = prob[j]
            dp = dot(vt[j], g)
            ds = (low.astype(jnp.float32) * (dp - delta)).astype(jnp.bfloat16)
            dv_acc[j] += dot_nt(gs, low)
            dk_acc[j] += dot_nt(qs, ds)
            dq += dot(kb[j], ds)
        dqb[row, :, cols] = (dq * (inv * scale)).astype(jnp.bfloat16)

        @pl.when(jnp.logical_and(turn == 0, sub == parts - 1))
        def _():
            for t in range(2):
                own_out(t).start()

        @pl.when(jnp.logical_and(turn > 0, sub == parts - 1))
        def _():
            for t in range(2):
                send_out(t, row).start()

        return carry

    lax.fori_loop(0, n * parts, step, 0)

    dkb[...] = dk_acc[...].astype(jnp.bfloat16)
    dvb[...] = dv_acc[...].astype(jnp.bfloat16)
    for off in offs:
        for t in (2, 3):
            send_out(t, other(off)).start()
    for t in (2, 3):
        own_out(t).start()
    for t in range(1, 4):
        for off in offs:
            send_in(t, off).wait_send()
    for t in range(4):
        own_out(t).wait()
        for off in offs:
            send_out(t, other(off)).wait_send()
            take_out(t, other(off)).wait_recv()


def place_kernel(*refs):
    ins, outs, sems = refs[:4], refs[4:8], refs[8]
    copies = [pltpu.make_async_copy(ins[t], outs[t], sems.at[t]) for t in range(4)]
    for copy in copies:
        copy.start()
    for copy in copies:
        copy.wait()


def place(results):
    anywhere = pl.BlockSpec(memory_space=pl.ANY)
    size = sum(r.size * 4 for r in results)
    return tuple(
        pl.pallas_call(
            place_kernel,
            out_shape=[jax.ShapeDtypeStruct(r.shape, r.dtype) for r in results],
            in_specs=[pl.BlockSpec(memory_space=pltpu.VMEM)] * 4,
            out_specs=[pl.BlockSpec(memory_space=pltpu.HBM)] * 4,
            scratch_shapes=[pltpu.SemaphoreType.DMA((4,))],
            cost_estimate=pl.CostEstimate(flops=0, bytes_accessed=size, transcendentals=0),
        )(*results)
    )


def swap_body(queries, keys, values, out_grad, flags, order):
    n = lax.axis_size("token")
    heads, dim, blk = queries.shape
    low = pltpu.VMEM((n, dim, blk), jnp.bfloat16)
    wide = pltpu.VMEM((n, dim, blk), jnp.float32)
    turned = pltpu.VMEM((n, blk, dim), jnp.bfloat16)
    anywhere = pl.BlockSpec(memory_space=pl.ANY)
    smem = pl.BlockSpec(memory_space=pltpu.SMEM)
    sems = pltpu.SemaphoreType.DMA((4, n))
    toks = n * blk
    return place(
        pl.pallas_call(
            functools.partial(swap_kernel, n),
            out_shape=[jax.ShapeDtypeStruct(queries.shape, jnp.bfloat16)] * 4,
            in_specs=[smem, smem] + [anywhere] * 4,
            out_specs=[anywhere] * 4,
            scratch_shapes=[low] * 4
            + [turned] * 2
            + [pltpu.VMEM((n, blk, SUB), jnp.float32), pltpu.VMEM((n, blk, SUB), jnp.bfloat16)]
            + [wide] * 2
            + [low] * 4
            + [sems] * 4,
            compiler_params=pltpu.CompilerParams(
                collective_id=0, has_side_effects=True, vmem_limit_bytes=60 * 1024 * 1024
            ),
            cost_estimate=pl.CostEstimate(
                flops=12 * dim * toks * toks, bytes_accessed=16 * heads * dim * blk,
                transcendentals=toks * toks,
            ),
        )(flags, order, queries, keys, values, out_grad)
    )


def body(queries, keys, values, out_grad, flags, order):
    n = lax.axis_size("token")
    heads, _, toks = queries.shape
    if n > 1 and n % 2 == 0 and heads == n and toks == BLK:
        return swap_body(queries, keys, values, out_grad, flags, order)
    return ring_body(queries, keys, values, out_grad, flags, order)


def solution(mesh):
    in_specs = (
        P(("image", "head"), None, "token"),
        P(("image", "head"), None, "token"),
        P(("image", "head"), None, "token"),
        P(("image", "head"), None, "token"),
        P(),
        P(),
    )
    out_specs = (
        P(("image", "head"), None, "token"),
        P(("image", "head"), None, "token"),
        P(("image", "head"), None, "token"),
        P(("image", "head"), None, "token"),
    )
    return jax.shard_map(body, mesh=mesh, in_specs=in_specs, out_specs=out_specs, check_vma=False)
```

```python
import functools

import jax
import jax.numpy as jnp
from jax import lax
from jax.experimental import pallas as pl
from jax.experimental.pallas import tpu as pltpu
from jax.sharding import PartitionSpec as P

BLK = 512


def from_behind(value, axis, steps):
    count = lax.axis_size(axis)
    pairs = [(source, (source + steps) % count) for source in range(count)]
    return lax.ppermute(value, axis, pairs)


def block_pairs(flags, order, query_dev, key_dev, per):
    nblk = order.shape[0]
    labels = jnp.arange(nblk, dtype=jnp.int32)[None, :]
    query_ids = lax.dynamic_slice_in_dim(order, query_dev * per, per)
    key_ids = lax.dynamic_slice_in_dim(order, key_dev * per, per)
    query_hot = (query_ids[:, None] == labels).astype(jnp.float32)
    key_hot = (key_ids[:, None] == labels).astype(jnp.float32)
    return jnp.dot(jnp.dot(query_hot, flags.astype(jnp.float32)), key_hot.T) > 0.5


def masked_scores(query, key, pairs, scale):
    score = jnp.einsum("hdi,hdj->hij", query, key, preferred_element_type=jnp.float32) * scale
    heads, rows, cols = score.shape
    per = pairs.shape[0]
    shaped = score.reshape(heads, per, rows // per, per, cols // per)
    shaped = jnp.where(pairs[None, :, None, :, None], shaped, -jnp.inf)
    return shaped.reshape(heads, rows, cols)


def forward_tile(query, key, value, state, pairs, scale):
    output, running_max, total = state
    score = masked_scores(query, key, pairs, scale)
    new_max = jnp.maximum(running_max, jnp.max(score, axis=2))
    safe_max = jnp.where(jnp.isfinite(new_max), new_max, 0.0)
    rescale = jnp.exp(running_max - safe_max)
    weight = jnp.exp(score - safe_max[..., None])
    total = total * rescale + jnp.sum(weight, axis=2)
    output = output * rescale[:, None, :] + jnp.einsum(
        "hij,hdj->hdi", weight.astype(jnp.bfloat16), value, preferred_element_type=jnp.float32
    )
    return (output, new_max, total)


def backward_tile(query, grad, lse, delta, key, value, pairs, scale):
    score = masked_scores(query, key, pairs, scale)
    prob = jnp.exp(score - lse[..., None])
    value_part = jnp.einsum(
        "hij,hdi->hdj", prob.astype(jnp.bfloat16), grad, preferred_element_type=jnp.float32
    )
    dprob = jnp.einsum("hdi,hdj->hij", grad, value, preferred_element_type=jnp.float32)
    dscore = (prob * (dprob - delta[..., None]) * scale).astype(jnp.bfloat16)
    key_part = jnp.einsum("hij,hdi->hdj", dscore, query, preferred_element_type=jnp.float32)
    query_part = jnp.einsum("hij,hdj->hdi", dscore, key, preferred_element_type=jnp.float32)
    return (query_part, key_part, value_part)


def ring_body(queries, keys, values, out_grad, flags, order):
    cycle = lax.axis_size("token")
    me = lax.axis_index("token")
    heads, dim, toks = queries.shape
    per = toks // BLK
    scale = dim ** (-0.5)
    zero_field = jnp.zeros((heads, dim, toks), jnp.float32)
    zero_rows = jnp.zeros((heads, toks), jnp.float32)
    start_max = jnp.full((heads, toks), -jnp.inf, jnp.float32)

    def forward_step(step, carry):
        visitor, output, running_max, total = carry
        source = (me - step) % cycle
        pairs = block_pairs(flags, order, source, me, per)
        state = lax.cond(
            jnp.any(pairs),
            lambda s: forward_tile(visitor, keys, values, s, pairs, scale),
            lambda s: s,
            (output, running_max, total),
        )
        visitor = from_behind(visitor, "token", 1)
        output, running_max, total = from_behind(state, "token", 1)
        return (visitor, output, running_max, total)

    _, output, running_max, total = lax.fori_loop(
        0, cycle, forward_step, (queries, zero_field, start_max, zero_rows)
    )
    state = (output, running_max, total)
    finish_output, finish_running_max, finish_total = state
    attended = (finish_output / finish_total[:, None, :]).astype(jnp.bfloat16)
    lse = finish_running_max + jnp.log(finish_total)
    delta = jnp.sum(out_grad.astype(jnp.float32) * attended.astype(jnp.float32), axis=1)
    attended, lse, delta = (attended, lse, delta)

    def backward_step(step, carry):
        visitor, grad, query_acc, lse_vis, delta_vis, key_acc, value_acc = carry
        source = (me - step) % cycle
        pairs = block_pairs(flags, order, source, me, per)

        def live(accs):
            query_part, key_part, value_part = backward_tile(
                visitor, grad, lse_vis, delta_vis, keys, values, pairs, scale
            )
            return (accs[0] + query_part, accs[1] + key_part, accs[2] + value_part)

        query_acc, key_acc, value_acc = lax.cond(
            jnp.any(pairs), live, lambda a: a, (query_acc, key_acc, value_acc)
        )
        visitor, grad = from_behind((visitor, grad), "token", 1)
        query_acc, lse_vis, delta_vis = from_behind((query_acc, lse_vis, delta_vis), "token", 1)
        return (visitor, grad, query_acc, lse_vis, delta_vis, key_acc, value_acc)

    final = lax.fori_loop(
        0, cycle, backward_step, (queries, out_grad, zero_field, lse, delta, zero_field, zero_field)
    )
    query_acc, key_acc, value_acc = (final[2], final[5], final[6])
    return (
        attended,
        query_acc.astype(jnp.bfloat16),
        key_acc.astype(jnp.bfloat16),
        value_acc.astype(jnp.bfloat16),
    )


LOG2E = 1.4426950408889634
SUB = 256


def dot(a, b):
    return jnp.dot(a, b, preferred_element_type=jnp.float32)


def crossed(a, b, n):
    out, w = 0, 1
    while w < n:
        out = out + w * lax.rem(lax.div(a, jnp.int32(w)) + lax.div(jnp.int32(b), jnp.int32(w)), jnp.int32(2))
        w *= 2
    return out


def swap_kernel(
    n, flags, order, q_in, k_in, v_in, g_in, o_out, dq_out, dk_out, dv_out,
    qb, kb, vb, gb, kt, vt, score, prob, dk_acc, dv_acc, ob, dqb, dkb, dvb,
    in_send, in_recv, out_send, out_recv,
):
    me = lax.axis_index("token")
    dim, blk = qb.shape[1:]
    scale = dim ** (-0.5)
    expo = scale * LOG2E
    ins = ((k_in, kb), (v_in, vb), (q_in, qb), (g_in, gb))
    outs = ((ob, o_out), (dqb, dq_out), (dkb, dk_out), (dvb, dv_out))
    offs = list(range(1, n))
    far = offs[n // 2 - 1:] + offs[:n // 2 - 1]

    def other(off):
        return crossed(me, off, n)

    def send_in(t, off):
        src, dst = ins[t]
        to = other(off)
        return pltpu.make_async_remote_copy(
            src_ref=src.at[to], dst_ref=dst.at[me], send_sem=in_send.at[t, off],
            recv_sem=in_recv.at[t, me], device_id={"token": to},
        )

    def take_in(t, frm):
        src, dst = ins[t]
        return pltpu.make_async_remote_copy(
            src_ref=src.at[me], dst_ref=dst.at[frm], send_sem=in_send.at[t, 0],
            recv_sem=in_recv.at[t, frm], device_id={"token": frm},
        )

    def own_in(t):
        src, dst = ins[t]
        return pltpu.make_async_copy(src.at[me], dst.at[me], in_recv.at[t, me])

    def send_out(t, to):
        src, dst = outs[t]
        return pltpu.make_async_remote_copy(
            src_ref=src.at[to], dst_ref=dst.at[me], send_sem=out_send.at[t, to],
            recv_sem=out_recv.at[t, me], device_id={"token": to},
        )

    def take_out(t, frm):
        src, dst = outs[t]
        return pltpu.make_async_remote_copy(
            src_ref=src.at[me], dst_ref=dst.at[frm], send_sem=out_send.at[t, me],
            recv_sem=out_recv.at[t, frm], device_id={"token": frm},
        )

    def own_out(t):
        src, dst = outs[t]
        return pltpu.make_async_copy(src.at[me], dst.at[me], out_recv.at[t, me])

    for t in range(4):
        own_in(t).start()
    barrier = pltpu.get_barrier_semaphore()
    for off in range(1, n):
        pl.semaphore_signal(barrier, inc=1, device_id={"token": other(off)})
    pl.semaphore_wait(barrier, n - 1)

    for t in range(2):
        for off in far:
            send_in(t, off).start()
    dk_acc[...] = jnp.zeros_like(dk_acc)
    dv_acc[...] = jnp.zeros_like(dv_acc)
    for t in range(4):
        own_in(t).wait()
    for off in offs:
        send_in(0, off).wait_send()
    for off in offs:
        for t in (2, 3):
            send_in(t, off).start()
    for off in offs:
        take_in(0, other(off)).wait_recv()
    for j in range(n):
        kt[j] = kb[j].astype(jnp.float32).T.astype(jnp.bfloat16)
    for off in offs:
        take_in(1, other(off)).wait_recv()
    for j in range(n):
        vt[j] = vb[j].astype(jnp.float32).T.astype(jnp.bfloat16)

    parts = blk // SUB

    def step(i, carry):
        turn, sub = lax.div(i, parts), lax.rem(i, parts)
        row = other(turn)
        cols = pl.ds(pl.multiple_of(sub * SUB, SUB), SUB)

        @pl.when(jnp.logical_and(turn > 0, sub == 0))
        def _():
            take_in(2, row).wait_recv()
            take_in(3, row).wait_recv()

        label = order[row]
        bias = [jnp.where(flags[label, order[j]] != 0, 0.0, -jnp.inf) for j in range(n)]
        q = qb[row, :, cols]
        g = gb[row, :, cols]
        top = None
        for j in range(n):
            s = dot(kt[j], q)
            score[j] = s
            m = jnp.max(s, axis=0, keepdims=True) + bias[j]
            top = m if top is None else jnp.maximum(top, m)
        top = top * expo
        total = jnp.zeros_like(top)
        o = jnp.zeros((dim, SUB), jnp.float32)
        for j in range(n):
            p = jnp.exp2(score[j] * expo - (top - bias[j]))
            total += jnp.sum(p, axis=0, keepdims=True)
            low = p.astype(jnp.bfloat16)
            prob[j] = low
            o += dot(vb[j], low)
        inv = 1.0 / total
        att = (o * inv).astype(jnp.bfloat16)
        ob[row, :, cols] = att
        gf = g.astype(jnp.float32)
        delta = jnp.sum(gf * att.astype(jnp.float32), axis=0, keepdims=True)
        gs = (gf * inv).T.astype(jnp.bfloat16)
        qs = (q.astype(jnp.float32) * (inv * scale)).T.astype(jnp.bfloat16)
        dq = jnp.zeros((dim, SUB), jnp.float32)
        for j in range(n):
            low = prob[j]
            dp = dot(vt[j], g)
            ds = (low.astype(jnp.float32) * (dp - delta)).astype(jnp.bfloat16)
            dv_acc[j] += dot(low, gs)
            dk_acc[j] += dot(ds, qs)
            dq += dot(kb[j], ds)
        dqb[row, :, cols] = (dq * (inv * scale)).astype(jnp.bfloat16)

        @pl.when(jnp.logical_and(turn == 0, sub == parts - 1))
        def _():
            for t in range(2):
                own_out(t).start()

        @pl.when(jnp.logical_and(turn > 0, sub == parts - 1))
        def _():
            for t in range(2):
                send_out(t, row).start()

        return carry

    lax.fori_loop(0, n * parts, step, 0)

    for j in range(n):
        dkb[j] = dk_acc[j].T.astype(jnp.bfloat16)
        dvb[j] = dv_acc[j].T.astype(jnp.bfloat16)
    for off in far:
        for t in (2, 3):
            send_out(t, other(off)).start()
    for t in (2, 3):
        own_out(t).start()
    for t in range(1, 4):
        for off in offs:
            send_in(t, off).wait_send()
    for t in range(4):
        own_out(t).wait()
        for off in offs:
            send_out(t, other(off)).wait_send()
            take_out(t, other(off)).wait_recv()


def place_kernel(*refs):
    ins, outs, sems = refs[:4], refs[4:8], refs[8]
    copies = [pltpu.make_async_copy(ins[t], outs[t], sems.at[t]) for t in range(4)]
    for copy in copies:
        copy.start()
    for copy in copies:
        copy.wait()


def place(results):
    anywhere = pl.BlockSpec(memory_space=pl.ANY)
    size = sum(r.size * 4 for r in results)
    return tuple(
        pl.pallas_call(
            place_kernel,
            out_shape=[jax.ShapeDtypeStruct(r.shape, r.dtype) for r in results],
            in_specs=[pl.BlockSpec(memory_space=pltpu.VMEM)] * 4,
            out_specs=[pl.BlockSpec(memory_space=pltpu.HBM)] * 4,
            scratch_shapes=[pltpu.SemaphoreType.DMA((4,))],
            cost_estimate=pl.CostEstimate(flops=0, bytes_accessed=size, transcendentals=0),
        )(*results)
    )


def swap_body(queries, keys, values, out_grad, flags, order):
    n = lax.axis_size("token")
    heads, dim, blk = queries.shape
    low = pltpu.VMEM((n, dim, blk), jnp.bfloat16)
    wide = pltpu.VMEM((n, blk, dim), jnp.float32)
    turned = pltpu.VMEM((n, blk, dim), jnp.bfloat16)
    anywhere = pl.BlockSpec(memory_space=pl.ANY)
    smem = pl.BlockSpec(memory_space=pltpu.SMEM)
    sems = pltpu.SemaphoreType.DMA((4, n))
    toks = n * blk
    return place(
        pl.pallas_call(
            functools.partial(swap_kernel, n),
            out_shape=[jax.ShapeDtypeStruct(queries.shape, jnp.bfloat16)] * 4,
            in_specs=[smem, smem] + [anywhere] * 4,
            out_specs=[anywhere] * 4,
            scratch_shapes=[low] * 4
            + [turned] * 2
            + [pltpu.VMEM((n, blk, SUB), jnp.float32), pltpu.VMEM((n, blk, SUB), jnp.bfloat16)]
            + [wide] * 2
            + [low] * 4
            + [sems] * 4,
            compiler_params=pltpu.CompilerParams(
                collective_id=0, has_side_effects=True, vmem_limit_bytes=60 * 1024 * 1024
            ),
            cost_estimate=pl.CostEstimate(
                flops=12 * dim * toks * toks, bytes_accessed=16 * heads * dim * blk,
                transcendentals=toks * toks,
            ),
        )(flags, order, queries, keys, values, out_grad)
    )


def body(queries, keys, values, out_grad, flags, order):
    n = lax.axis_size("token")
    heads, _, toks = queries.shape
    if n > 1 and n & (n - 1) == 0 and heads == n and toks == BLK:
        return swap_body(queries, keys, values, out_grad, flags, order)
    return ring_body(queries, keys, values, out_grad, flags, order)


def solution(mesh):
    in_specs = (
        P(("image", "head"), None, "token"),
        P(("image", "head"), None, "token"),
        P(("image", "head"), None, "token"),
        P(("image", "head"), None, "token"),
        P(),
        P(),
    )
    out_specs = (
        P(("image", "head"), None, "token"),
        P(("image", "head"), None, "token"),
        P(("image", "head"), None, "token"),
        P(("image", "head"), None, "token"),
    )
    return jax.shard_map(body, mesh=mesh, in_specs=in_specs, out_specs=out_specs, check_vma=False)
```

```python
import functools

import jax
import jax.numpy as jnp
from jax import lax
from jax.experimental import pallas as pl
from jax.experimental.pallas import tpu as pltpu
from jax.sharding import PartitionSpec as P

BLK = 512


def from_behind(value, axis, steps):
    count = lax.axis_size(axis)
    pairs = [(source, (source + steps) % count) for source in range(count)]
    return lax.ppermute(value, axis, pairs)


def block_pairs(flags, order, query_dev, key_dev, per):
    nblk = order.shape[0]
    labels = jnp.arange(nblk, dtype=jnp.int32)[None, :]
    query_ids = lax.dynamic_slice_in_dim(order, query_dev * per, per)
    key_ids = lax.dynamic_slice_in_dim(order, key_dev * per, per)
    query_hot = (query_ids[:, None] == labels).astype(jnp.float32)
    key_hot = (key_ids[:, None] == labels).astype(jnp.float32)
    return jnp.dot(jnp.dot(query_hot, flags.astype(jnp.float32)), key_hot.T) > 0.5


def masked_scores(query, key, pairs, scale):
    score = jnp.einsum("hdi,hdj->hij", query, key, preferred_element_type=jnp.float32) * scale
    heads, rows, cols = score.shape
    per = pairs.shape[0]
    shaped = score.reshape(heads, per, rows // per, per, cols // per)
    shaped = jnp.where(pairs[None, :, None, :, None], shaped, -jnp.inf)
    return shaped.reshape(heads, rows, cols)


def forward_tile(query, key, value, state, pairs, scale):
    output, running_max, total = state
    score = masked_scores(query, key, pairs, scale)
    new_max = jnp.maximum(running_max, jnp.max(score, axis=2))
    safe_max = jnp.where(jnp.isfinite(new_max), new_max, 0.0)
    rescale = jnp.exp(running_max - safe_max)
    weight = jnp.exp(score - safe_max[..., None])
    total = total * rescale + jnp.sum(weight, axis=2)
    output = output * rescale[:, None, :] + jnp.einsum(
        "hij,hdj->hdi", weight.astype(jnp.bfloat16), value, preferred_element_type=jnp.float32
    )
    return (output, new_max, total)


def backward_tile(query, grad, lse, delta, key, value, pairs, scale):
    score = masked_scores(query, key, pairs, scale)
    prob = jnp.exp(score - lse[..., None])
    value_part = jnp.einsum(
        "hij,hdi->hdj", prob.astype(jnp.bfloat16), grad, preferred_element_type=jnp.float32
    )
    dprob = jnp.einsum("hdi,hdj->hij", grad, value, preferred_element_type=jnp.float32)
    dscore = (prob * (dprob - delta[..., None]) * scale).astype(jnp.bfloat16)
    key_part = jnp.einsum("hij,hdi->hdj", dscore, query, preferred_element_type=jnp.float32)
    query_part = jnp.einsum("hij,hdj->hdi", dscore, key, preferred_element_type=jnp.float32)
    return (query_part, key_part, value_part)


def ring_body(queries, keys, values, out_grad, flags, order):
    cycle = lax.axis_size("token")
    me = lax.axis_index("token")
    heads, dim, toks = queries.shape
    per = toks // BLK
    scale = dim ** (-0.5)
    zero_field = jnp.zeros((heads, dim, toks), jnp.float32)
    zero_rows = jnp.zeros((heads, toks), jnp.float32)
    start_max = jnp.full((heads, toks), -jnp.inf, jnp.float32)

    def forward_step(step, carry):
        visitor, output, running_max, total = carry
        source = (me - step) % cycle
        pairs = block_pairs(flags, order, source, me, per)
        state = lax.cond(
            jnp.any(pairs),
            lambda s: forward_tile(visitor, keys, values, s, pairs, scale),
            lambda s: s,
            (output, running_max, total),
        )
        visitor = from_behind(visitor, "token", 1)
        output, running_max, total = from_behind(state, "token", 1)
        return (visitor, output, running_max, total)

    _, output, running_max, total = lax.fori_loop(
        0, cycle, forward_step, (queries, zero_field, start_max, zero_rows)
    )
    state = (output, running_max, total)
    finish_output, finish_running_max, finish_total = state
    attended = (finish_output / finish_total[:, None, :]).astype(jnp.bfloat16)
    lse = finish_running_max + jnp.log(finish_total)
    delta = jnp.sum(out_grad.astype(jnp.float32) * attended.astype(jnp.float32), axis=1)
    attended, lse, delta = (attended, lse, delta)

    def backward_step(step, carry):
        visitor, grad, query_acc, lse_vis, delta_vis, key_acc, value_acc = carry
        source = (me - step) % cycle
        pairs = block_pairs(flags, order, source, me, per)

        def live(accs):
            query_part, key_part, value_part = backward_tile(
                visitor, grad, lse_vis, delta_vis, keys, values, pairs, scale
            )
            return (accs[0] + query_part, accs[1] + key_part, accs[2] + value_part)

        query_acc, key_acc, value_acc = lax.cond(
            jnp.any(pairs), live, lambda a: a, (query_acc, key_acc, value_acc)
        )
        visitor, grad = from_behind((visitor, grad), "token", 1)
        query_acc, lse_vis, delta_vis = from_behind((query_acc, lse_vis, delta_vis), "token", 1)
        return (visitor, grad, query_acc, lse_vis, delta_vis, key_acc, value_acc)

    final = lax.fori_loop(
        0, cycle, backward_step, (queries, out_grad, zero_field, lse, delta, zero_field, zero_field)
    )
    query_acc, key_acc, value_acc = (final[2], final[5], final[6])
    return (
        attended,
        query_acc.astype(jnp.bfloat16),
        key_acc.astype(jnp.bfloat16),
        value_acc.astype(jnp.bfloat16),
    )


LOG2E = 1.4426950408889634
SUB = 512


def dot(a, b):
    return jnp.dot(a, b, preferred_element_type=jnp.float32)


def crossed(a, b, n):
    out, w = 0, 1
    while w < n:
        out = out + w * lax.rem(lax.div(a, jnp.int32(w)) + lax.div(jnp.int32(b), jnp.int32(w)), jnp.int32(2))
        w *= 2
    return out


def swap_kernel(
    n, flags_in, order_in, q_in, k_in, v_in, g_in, o_out, dq_out, dk_out, dv_out,
    qb, kb, vb, gb, kt, vt, score, prob, dk_acc, dv_acc, ob, dqb, dkb, dvb,
    in_send, in_recv, out_send, out_recv, flags, order, table_sem,
):
    me = lax.axis_index("token")
    dim, blk = qb.shape[1:]
    scale = dim ** (-0.5)
    expo = scale * LOG2E
    ins = ((k_in, kb), (v_in, vb), (q_in, qb), (g_in, gb))
    outs = ((ob, o_out), (dqb, dq_out), (dkb, dk_out), (dvb, dv_out))
    offs = list(range(1, n))
    far = offs[n // 2 - 1:] + offs[:n // 2 - 1]

    def other(off):
        return crossed(me, off, n)

    def send_in(t, off):
        src, dst = ins[t]
        to = other(off)
        return pltpu.make_async_remote_copy(
            src_ref=src.at[to], dst_ref=dst.at[me], send_sem=in_send.at[t, off],
            recv_sem=in_recv.at[t, me], device_id={"token": to},
        )

    def take_in(t, frm):
        src, dst = ins[t]
        return pltpu.make_async_remote_copy(
            src_ref=src.at[me], dst_ref=dst.at[frm], send_sem=in_send.at[t, 0],
            recv_sem=in_recv.at[t, frm], device_id={"token": frm},
        )

    def own_in(t):
        src, dst = ins[t]
        return pltpu.make_async_copy(src.at[me], dst.at[me], in_recv.at[t, me])

    def send_out(t, to):
        src, dst = outs[t]
        return pltpu.make_async_remote_copy(
            src_ref=src.at[to], dst_ref=dst.at[me], send_sem=out_send.at[t, to],
            recv_sem=out_recv.at[t, me], device_id={"token": to},
        )

    def take_out(t, frm):
        src, dst = outs[t]
        return pltpu.make_async_remote_copy(
            src_ref=src.at[me], dst_ref=dst.at[frm], send_sem=out_send.at[t, me],
            recv_sem=out_recv.at[t, frm], device_id={"token": frm},
        )

    def own_out(t):
        src, dst = outs[t]
        return pltpu.make_async_copy(src.at[me], dst.at[me], out_recv.at[t, me])

    barrier = pltpu.get_barrier_semaphore()
    for off in range(1, n):
        pl.semaphore_signal(barrier, inc=1, device_id={"token": other(off)})
    tables = [
        pltpu.make_async_copy(flags_in, flags, table_sem.at[0]),
        pltpu.make_async_copy(order_in, order, table_sem.at[1]),
    ]
    for copy in tables:
        copy.start()
    for t in range(4):
        own_in(t).start()
    pl.semaphore_wait(barrier, n - 1)

    for t in range(2):
        for off in far:
            send_in(t, off).start()
    dk_acc[...] = jnp.zeros_like(dk_acc)
    dv_acc[...] = jnp.zeros_like(dv_acc)
    for copy in tables:
        copy.wait()
    for t in range(4):
        own_in(t).wait()
    for off in offs:
        send_in(0, off).wait_send()
    for off in offs:
        for t in (2, 3):
            send_in(t, off).start()
    for off in offs:
        take_in(0, other(off)).wait_recv()
    for j in range(n):
        kt[j] = kb[j].astype(jnp.float32).T.astype(jnp.bfloat16)
    for off in offs:
        take_in(1, other(off)).wait_recv()
    for j in range(n):
        vt[j] = vb[j].astype(jnp.float32).T.astype(jnp.bfloat16)

    parts = blk // SUB

    def step(i, carry):
        turn, sub = lax.div(i, parts), lax.rem(i, parts)
        row = other(turn)
        cols = pl.ds(pl.multiple_of(sub * SUB, SUB), SUB)

        @pl.when(jnp.logical_and(turn > 0, sub == 0))
        def _():
            take_in(2, row).wait_recv()
            take_in(3, row).wait_recv()

        label = order[row]
        bias = [jnp.where(flags[label, order[j]] != 0, 0.0, -jnp.inf) for j in range(n)]
        q = qb[row, :, cols]
        g = gb[row, :, cols]
        top = None
        for j in range(n):
            s = dot(kt[j], q)
            score[j] = s
            m = jnp.max(s, axis=0, keepdims=True) + bias[j]
            top = m if top is None else jnp.maximum(top, m)
        top = top * expo
        total = jnp.zeros_like(top)
        o = jnp.zeros((dim, SUB), jnp.float32)
        for j in range(n):
            p = jnp.exp2(score[j] * expo - (top - bias[j]))
            total += jnp.sum(p, axis=0, keepdims=True)
            low = p.astype(jnp.bfloat16)
            prob[j] = low
            o += dot(vb[j], low)
        inv = 1.0 / total
        att = (o * inv).astype(jnp.bfloat16)
        ob[row, :, cols] = att
        gf = g.astype(jnp.float32)
        delta = jnp.sum(gf * att.astype(jnp.float32), axis=0, keepdims=True)
        gs = (gf * inv).T.astype(jnp.bfloat16)
        qs = (q.astype(jnp.float32) * (inv * scale)).T.astype(jnp.bfloat16)
        dq = jnp.zeros((dim, SUB), jnp.float32)
        for j in range(n):
            low = prob[j]
            dp = dot(vt[j], g)
            ds = (low.astype(jnp.float32) * (dp - delta)).astype(jnp.bfloat16)
            dv_acc[j] += dot(low, gs)
            dk_acc[j] += dot(ds, qs)
            dq += dot(kb[j], ds)
        dqb[row, :, cols] = (dq * (inv * scale)).astype(jnp.bfloat16)

        @pl.when(jnp.logical_and(turn == 0, sub == parts - 1))
        def _():
            for t in range(2):
                own_out(t).start()

        @pl.when(jnp.logical_and(turn > 0, sub == parts - 1))
        def _():
            for t in range(2):
                send_out(t, row).start()

        return carry

    lax.fori_loop(0, n * parts, step, 0)

    for j in range(n):
        dkb[j] = dk_acc[j].T.astype(jnp.bfloat16)
        dvb[j] = dv_acc[j].T.astype(jnp.bfloat16)
    for off in far:
        for t in (2, 3):
            send_out(t, other(off)).start()
    for t in (2, 3):
        own_out(t).start()
    for t in range(1, 4):
        for off in offs:
            send_in(t, off).wait_send()
    for t in range(4):
        own_out(t).wait()
        for off in offs:
            send_out(t, other(off)).wait_send()
            take_out(t, other(off)).wait_recv()


def place_kernel(*refs):
    ins, outs, sems = refs[:4], refs[4:8], refs[8]
    copies = [pltpu.make_async_copy(ins[t], outs[t], sems.at[t]) for t in range(4)]
    for copy in copies:
        copy.start()
    for copy in copies:
        copy.wait()


def place(results):
    anywhere = pl.BlockSpec(memory_space=pl.ANY)
    size = sum(r.size * 4 for r in results)
    return tuple(
        pl.pallas_call(
            place_kernel,
            out_shape=[jax.ShapeDtypeStruct(r.shape, r.dtype) for r in results],
            in_specs=[pl.BlockSpec(memory_space=pltpu.VMEM)] * 4,
            out_specs=[pl.BlockSpec(memory_space=pltpu.HBM)] * 4,
            scratch_shapes=[pltpu.SemaphoreType.DMA((4,))],
            cost_estimate=pl.CostEstimate(flops=0, bytes_accessed=size, transcendentals=0),
        )(*[pltpu.with_memory_space_constraint(r, pltpu.VMEM) for r in results])
    )


def swap_body(queries, keys, values, out_grad, flags, order):
    n = lax.axis_size("token")
    heads, dim, blk = queries.shape
    low = pltpu.VMEM((n, dim, blk), jnp.bfloat16)
    wide = pltpu.VMEM((n, blk, dim), jnp.float32)
    turned = pltpu.VMEM((n, blk, dim), jnp.bfloat16)
    anywhere = pl.BlockSpec(memory_space=pl.ANY)
    sems = pltpu.SemaphoreType.DMA((4, n))
    toks = n * blk
    return place(
        pl.pallas_call(
            functools.partial(swap_kernel, n),
            out_shape=[pltpu.VMEM(queries.shape, jnp.bfloat16)] * 4,
            in_specs=[anywhere] * 6,
            out_specs=[pl.BlockSpec(memory_space=pltpu.VMEM)] * 4,
            scratch_shapes=[low] * 4
            + [turned] * 2
            + [pltpu.VMEM((n, blk, SUB), jnp.float32), pltpu.VMEM((n, blk, SUB), jnp.bfloat16)]
            + [wide] * 2
            + [low] * 4
            + [sems] * 4
            + [pltpu.SMEM(flags.shape, jnp.int32), pltpu.SMEM(order.shape, jnp.int32)]
            + [pltpu.SemaphoreType.DMA((2,))],
            compiler_params=pltpu.CompilerParams(
                collective_id=0, has_side_effects=True, vmem_limit_bytes=60 * 1024 * 1024
            ),
            cost_estimate=pl.CostEstimate(
                flops=12 * dim * toks * toks, bytes_accessed=16 * heads * dim * blk,
                transcendentals=toks * toks,
            ),
        )(flags, order, queries, keys, values, out_grad)
    )


def body(queries, keys, values, out_grad, flags, order):
    n = lax.axis_size("token")
    heads, _, toks = queries.shape
    if n > 1 and n & (n - 1) == 0 and heads == n and toks == BLK:
        return swap_body(queries, keys, values, out_grad, flags, order)
    return ring_body(queries, keys, values, out_grad, flags, order)


def solution(mesh):
    in_specs = (
        P(("image", "head"), None, "token"),
        P(("image", "head"), None, "token"),
        P(("image", "head"), None, "token"),
        P(("image", "head"), None, "token"),
        P(),
        P(),
    )
    out_specs = (
        P(("image", "head"), None, "token"),
        P(("image", "head"), None, "token"),
        P(("image", "head"), None, "token"),
        P(("image", "head"), None, "token"),
    )
    return jax.shard_map(body, mesh=mesh, in_specs=in_specs, out_specs=out_specs, check_vma=False)
```

```python
import functools

import jax
import jax.numpy as jnp
from jax import lax
from jax.experimental import pallas as pl
from jax.experimental.pallas import tpu as pltpu
from jax.sharding import PartitionSpec as P

BLK = 512


def from_behind(value, axis, steps):
    count = lax.axis_size(axis)
    pairs = [(source, (source + steps) % count) for source in range(count)]
    return lax.ppermute(value, axis, pairs)


def block_pairs(flags, order, query_dev, key_dev, per):
    nblk = order.shape[0]
    labels = jnp.arange(nblk, dtype=jnp.int32)[None, :]
    query_ids = lax.dynamic_slice_in_dim(order, query_dev * per, per)
    key_ids = lax.dynamic_slice_in_dim(order, key_dev * per, per)
    query_hot = (query_ids[:, None] == labels).astype(jnp.float32)
    key_hot = (key_ids[:, None] == labels).astype(jnp.float32)
    return jnp.dot(jnp.dot(query_hot, flags.astype(jnp.float32)), key_hot.T) > 0.5


def masked_scores(query, key, pairs, scale):
    score = jnp.einsum("hdi,hdj->hij", query, key, preferred_element_type=jnp.float32) * scale
    heads, rows, cols = score.shape
    per = pairs.shape[0]
    shaped = score.reshape(heads, per, rows // per, per, cols // per)
    shaped = jnp.where(pairs[None, :, None, :, None], shaped, -jnp.inf)
    return shaped.reshape(heads, rows, cols)


def forward_tile(query, key, value, state, pairs, scale):
    output, running_max, total = state
    score = masked_scores(query, key, pairs, scale)
    new_max = jnp.maximum(running_max, jnp.max(score, axis=2))
    safe_max = jnp.where(jnp.isfinite(new_max), new_max, 0.0)
    rescale = jnp.exp(running_max - safe_max)
    weight = jnp.exp(score - safe_max[..., None])
    total = total * rescale + jnp.sum(weight, axis=2)
    output = output * rescale[:, None, :] + jnp.einsum(
        "hij,hdj->hdi", weight.astype(jnp.bfloat16), value, preferred_element_type=jnp.float32
    )
    return (output, new_max, total)


def backward_tile(query, grad, lse, delta, key, value, pairs, scale):
    score = masked_scores(query, key, pairs, scale)
    prob = jnp.exp(score - lse[..., None])
    value_part = jnp.einsum(
        "hij,hdi->hdj", prob.astype(jnp.bfloat16), grad, preferred_element_type=jnp.float32
    )
    dprob = jnp.einsum("hdi,hdj->hij", grad, value, preferred_element_type=jnp.float32)
    dscore = (prob * (dprob - delta[..., None]) * scale).astype(jnp.bfloat16)
    key_part = jnp.einsum("hij,hdi->hdj", dscore, query, preferred_element_type=jnp.float32)
    query_part = jnp.einsum("hij,hdj->hdi", dscore, key, preferred_element_type=jnp.float32)
    return (query_part, key_part, value_part)


def ring_body(queries, keys, values, out_grad, flags, order):
    cycle = lax.axis_size("token")
    me = lax.axis_index("token")
    heads, dim, toks = queries.shape
    per = toks // BLK
    scale = dim ** (-0.5)
    zero_field = jnp.zeros((heads, dim, toks), jnp.float32)
    zero_rows = jnp.zeros((heads, toks), jnp.float32)
    start_max = jnp.full((heads, toks), -jnp.inf, jnp.float32)

    def forward_step(step, carry):
        visitor, output, running_max, total = carry
        source = (me - step) % cycle
        pairs = block_pairs(flags, order, source, me, per)
        state = lax.cond(
            jnp.any(pairs),
            lambda s: forward_tile(visitor, keys, values, s, pairs, scale),
            lambda s: s,
            (output, running_max, total),
        )
        visitor = from_behind(visitor, "token", 1)
        output, running_max, total = from_behind(state, "token", 1)
        return (visitor, output, running_max, total)

    _, output, running_max, total = lax.fori_loop(
        0, cycle, forward_step, (queries, zero_field, start_max, zero_rows)
    )
    state = (output, running_max, total)
    finish_output, finish_running_max, finish_total = state
    attended = (finish_output / finish_total[:, None, :]).astype(jnp.bfloat16)
    lse = finish_running_max + jnp.log(finish_total)
    delta = jnp.sum(out_grad.astype(jnp.float32) * attended.astype(jnp.float32), axis=1)
    attended, lse, delta = (attended, lse, delta)

    def backward_step(step, carry):
        visitor, grad, query_acc, lse_vis, delta_vis, key_acc, value_acc = carry
        source = (me - step) % cycle
        pairs = block_pairs(flags, order, source, me, per)

        def live(accs):
            query_part, key_part, value_part = backward_tile(
                visitor, grad, lse_vis, delta_vis, keys, values, pairs, scale
            )
            return (accs[0] + query_part, accs[1] + key_part, accs[2] + value_part)

        query_acc, key_acc, value_acc = lax.cond(
            jnp.any(pairs), live, lambda a: a, (query_acc, key_acc, value_acc)
        )
        visitor, grad = from_behind((visitor, grad), "token", 1)
        query_acc, lse_vis, delta_vis = from_behind((query_acc, lse_vis, delta_vis), "token", 1)
        return (visitor, grad, query_acc, lse_vis, delta_vis, key_acc, value_acc)

    final = lax.fori_loop(
        0, cycle, backward_step, (queries, out_grad, zero_field, lse, delta, zero_field, zero_field)
    )
    query_acc, key_acc, value_acc = (final[2], final[5], final[6])
    return (
        attended,
        query_acc.astype(jnp.bfloat16),
        key_acc.astype(jnp.bfloat16),
        value_acc.astype(jnp.bfloat16),
    )


LOG2E = 1.4426950408889634
SUB = 512


def dot(a, b):
    return jnp.dot(a, b, preferred_element_type=jnp.float32)


def crossed(a, b, n):
    out, w = 0, 1
    while w < n:
        out = out + w * lax.rem(lax.div(a, jnp.int32(w)) + lax.div(jnp.int32(b), jnp.int32(w)), jnp.int32(2))
        w *= 2
    return out


def swap_kernel(
    n, flags_in, order_in, q_in, k_in, v_in, g_in, o_out, dq_out, dk_out, dv_out,
    qb, kb, vb, gb, kt, vt, score, prob, dk_acc, dv_acc, ob, dqb, dkb, dvb,
    in_send, in_recv, out_send, out_recv, flags, order, table_sem,
):
    me = lax.axis_index("token")
    dim, blk = qb.shape[1:]
    scale = dim ** (-0.5)
    expo = scale * LOG2E
    ins = ((k_in, kb), (v_in, vb), (q_in, qb), (g_in, gb))
    outs = ((ob, o_out), (dqb, dq_out), (dkb, dk_out), (dvb, dv_out))
    offs = list(range(1, n))
    far = offs[n // 2 - 1:] + offs[:n // 2 - 1]

    def other(off):
        return crossed(me, off, n)

    def send_in(t, off):
        src, dst = ins[t]
        to = other(off)
        return pltpu.make_async_remote_copy(
            src_ref=src.at[to], dst_ref=dst.at[me], send_sem=in_send.at[t, off],
            recv_sem=in_recv.at[t, me], device_id={"token": to},
        )

    def take_in(t, frm):
        src, dst = ins[t]
        return pltpu.make_async_remote_copy(
            src_ref=src.at[me], dst_ref=dst.at[frm], send_sem=in_send.at[t, 0],
            recv_sem=in_recv.at[t, frm], device_id={"token": frm},
        )

    def own_in(t):
        src, dst = ins[t]
        return pltpu.make_async_copy(src.at[me], dst.at[me], in_recv.at[t, me])

    def send_out(t, to):
        src, dst = outs[t]
        return pltpu.make_async_remote_copy(
            src_ref=src.at[to], dst_ref=dst.at[me], send_sem=out_send.at[t, to],
            recv_sem=out_recv.at[t, me], device_id={"token": to},
        )

    def take_out(t, frm):
        src, dst = outs[t]
        return pltpu.make_async_remote_copy(
            src_ref=src.at[me], dst_ref=dst.at[frm], send_sem=out_send.at[t, me],
            recv_sem=out_recv.at[t, frm], device_id={"token": frm},
        )

    def own_out(t):
        src, dst = outs[t]
        return pltpu.make_async_copy(src.at[me], dst.at[me], out_recv.at[t, me])

    barrier = pltpu.get_barrier_semaphore()
    for off in range(1, n):
        pl.semaphore_signal(barrier, inc=1, device_id={"token": other(off)})
    tables = [
        pltpu.make_async_copy(flags_in, flags, table_sem.at[0]),
        pltpu.make_async_copy(order_in, order, table_sem.at[1]),
    ]
    for copy in tables:
        copy.start()
    for t in range(4):
        own_in(t).start()
    pl.semaphore_wait(barrier, n - 1)

    for t in range(2):
        for off in far:
            send_in(t, off).start()
    dk_acc[...] = jnp.zeros_like(dk_acc)
    dv_acc[...] = jnp.zeros_like(dv_acc)
    for copy in tables:
        copy.wait()
    for t in range(4):
        own_in(t).wait()
    for off in offs:
        send_in(0, off).wait_send()
    for off in offs:
        for t in (2, 3):
            send_in(t, off).start()
    for off in offs:
        take_in(0, other(off)).wait_recv()
    for j in range(n):
        kt[j] = kb[j].astype(jnp.float32).T.astype(jnp.bfloat16)

    parts = blk // SUB

    def step(i, carry):
        turn, sub = lax.div(i, parts), lax.rem(i, parts)
        row = other(turn)
        cols = pl.ds(pl.multiple_of(sub * SUB, SUB), SUB)

        @pl.when(jnp.logical_and(turn > 0, sub == 0))
        def _():
            take_in(2, row).wait_recv()
            take_in(3, row).wait_recv()

        label = order[row]
        bias = [jnp.where(flags[label, order[j]] != 0, 0.0, -jnp.inf) for j in range(n)]
        q = qb[row, :, cols]
        g = gb[row, :, cols]
        top = None
        for j in range(n):
            s = dot(kt[j], q)
            score[j] = s
            m = jnp.max(s, axis=0, keepdims=True) + bias[j]
            top = m if top is None else jnp.maximum(top, m)

        @pl.when(i == 0)
        def _():
            for near in offs:
                take_in(1, other(near)).wait_recv()
            for j in range(n):
                vt[j] = vb[j].astype(jnp.float32).T.astype(jnp.bfloat16)

        top = top * expo
        total = jnp.zeros_like(top)
        o = jnp.zeros((dim, SUB), jnp.float32)
        for j in range(n):
            p = jnp.exp2(score[j] * expo - (top - bias[j]))
            total += jnp.sum(p, axis=0, keepdims=True)
            low = p.astype(jnp.bfloat16)
            prob[j] = low
            o += dot(vb[j], low)
        inv = 1.0 / total
        att = (o * inv).astype(jnp.bfloat16)
        ob[row, :, cols] = att
        gf = g.astype(jnp.float32)
        delta = jnp.sum(gf * att.astype(jnp.float32), axis=0, keepdims=True)
        gs = (gf * inv).T.astype(jnp.bfloat16)
        qs = (q.astype(jnp.float32) * (inv * scale)).T.astype(jnp.bfloat16)
        dq = jnp.zeros((dim, SUB), jnp.float32)
        for j in range(n):
            low = prob[j]
            dp = dot(vt[j], g)
            ds = (low.astype(jnp.float32) * (dp - delta)).astype(jnp.bfloat16)
            dv_acc[j] += dot(low, gs)
            dk_acc[j] += dot(ds, qs)
            dq += dot(kb[j], ds)
        dqb[row, :, cols] = (dq * (inv * scale)).astype(jnp.bfloat16)

        @pl.when(jnp.logical_and(turn == 0, sub == parts - 1))
        def _():
            for t in range(2):
                own_out(t).start()

        @pl.when(jnp.logical_and(turn > 0, sub == parts - 1))
        def _():
            for t in range(2):
                send_out(t, row).start()

        return carry

    lax.fori_loop(0, n * parts, step, 0)

    for j in range(n):
        dkb[j] = dk_acc[j].T.astype(jnp.bfloat16)
        dvb[j] = dv_acc[j].T.astype(jnp.bfloat16)
    for off in far:
        for t in (2, 3):
            send_out(t, other(off)).start()
    for t in (2, 3):
        own_out(t).start()
    for t in range(1, 4):
        for off in offs:
            send_in(t, off).wait_send()
    for t in range(4):
        own_out(t).wait()
        for off in offs:
            send_out(t, other(off)).wait_send()
            take_out(t, other(off)).wait_recv()


def place_kernel(*refs):
    ins, outs, sems = refs[:4], refs[4:8], refs[8]
    copies = [pltpu.make_async_copy(ins[t], outs[t], sems.at[t]) for t in range(4)]
    for copy in copies:
        copy.start()
    for copy in copies:
        copy.wait()


def place(results):
    anywhere = pl.BlockSpec(memory_space=pl.ANY)
    size = sum(r.size * 4 for r in results)
    return tuple(
        pl.pallas_call(
            place_kernel,
            out_shape=[jax.ShapeDtypeStruct(r.shape, r.dtype) for r in results],
            in_specs=[pl.BlockSpec(memory_space=pltpu.VMEM)] * 4,
            out_specs=[pl.BlockSpec(memory_space=pltpu.HBM)] * 4,
            scratch_shapes=[pltpu.SemaphoreType.DMA((4,))],
            cost_estimate=pl.CostEstimate(flops=0, bytes_accessed=size, transcendentals=0),
        )(*[pltpu.with_memory_space_constraint(r, pltpu.VMEM) for r in results])
    )


def swap_body(queries, keys, values, out_grad, flags, order):
    n = lax.axis_size("token")
    heads, dim, blk = queries.shape
    low = pltpu.VMEM((n, dim, blk), jnp.bfloat16)
    wide = pltpu.VMEM((n, blk, dim), jnp.float32)
    turned = pltpu.VMEM((n, blk, dim), jnp.bfloat16)
    anywhere = pl.BlockSpec(memory_space=pl.ANY)
    sems = pltpu.SemaphoreType.DMA((4, n))
    toks = n * blk
    return place(
        pl.pallas_call(
            functools.partial(swap_kernel, n),
            out_shape=[pltpu.VMEM(queries.shape, jnp.bfloat16)] * 4,
            in_specs=[anywhere] * 6,
            out_specs=[pl.BlockSpec(memory_space=pltpu.VMEM)] * 4,
            scratch_shapes=[low] * 4
            + [turned] * 2
            + [pltpu.VMEM((n, blk, SUB), jnp.float32), pltpu.VMEM((n, blk, SUB), jnp.bfloat16)]
            + [wide] * 2
            + [low] * 4
            + [sems] * 4
            + [pltpu.SMEM(flags.shape, jnp.int32), pltpu.SMEM(order.shape, jnp.int32)]
            + [pltpu.SemaphoreType.DMA((2,))],
            compiler_params=pltpu.CompilerParams(
                collective_id=0, has_side_effects=True, vmem_limit_bytes=60 * 1024 * 1024
            ),
            cost_estimate=pl.CostEstimate(
                flops=12 * dim * toks * toks, bytes_accessed=16 * heads * dim * blk,
                transcendentals=toks * toks,
            ),
        )(flags, order, queries, keys, values, out_grad)
    )


def body(queries, keys, values, out_grad, flags, order):
    n = lax.axis_size("token")
    heads, _, toks = queries.shape
    if n > 1 and n & (n - 1) == 0 and heads == n and toks == BLK:
        return swap_body(queries, keys, values, out_grad, flags, order)
    return ring_body(queries, keys, values, out_grad, flags, order)


def solution(mesh):
    in_specs = (
        P(("image", "head"), None, "token"),
        P(("image", "head"), None, "token"),
        P(("image", "head"), None, "token"),
        P(("image", "head"), None, "token"),
        P(),
        P(),
    )
    out_specs = (
        P(("image", "head"), None, "token"),
        P(("image", "head"), None, "token"),
        P(("image", "head"), None, "token"),
        P(("image", "head"), None, "token"),
    )
    return jax.shard_map(body, mesh=mesh, in_specs=in_specs, out_specs=out_specs, check_vma=False)
```
